256 devices in a mesh: seq: 16 (over z, x_hi), head: 16 (over y, x_lo, core).
Axes of the slice: x: 4 (x_hi: 2, x_lo: 2; x = x_hi * 2 + x_lo), y: 4, z: 8, core: 2. Of those that a mesh axis runs over, the one named last changes fastest.
Arguments:
- q_latent: bfloat16 [2048, 1536], P('seq'), may hold values from -6 to 6
- kv_new: bfloat16 [2048, 576], P('seq'), may hold values from -6 to 6
- cache: bfloat16 [3072, 576], P('seq'), may hold values from -56 to 56
- latent_gain: float32 [512], replicated, may hold values from 0.1 to 1.9
- positions: int32 [2048], P('seq'), may hold values from 0 to 2047, as said below
- w_uq: bfloat16 [1536, 24576], P(None, 'head'), may hold values from -0.15625 to 0.15625
- w_uk: bfloat16 [128, 128, 512], P('head'), may hold values from -0.5 to 0.5
- w_uv: bfloat16 [128, 512, 128], P('head'), may hold values from -1 to 1
- w_out: bfloat16 [16384, 7168], P('head', 'seq'), may hold values from -0.1875 to 0.1875
Outputs:
- attended: bfloat16 [2048, 7168], P('seq', 'head')
The draws below stay inside these ranges and needn't reach their ends.
Inputs may be any that keep to these rules, and one draw needn't show every extreme that they name: positions holds every number below 2048 once; each aligned block of 64 rows holds consecutive rising numbers starting at a multiple of 64.
All inputs are finite; a program needn't handle non-finite values.
Results may differ from the reference program's by a relative error of at most 0.025.
Values may be sent and summed in bfloat16 or wider, within the bound.
No kernel may reach another device: no remote copies, remote signals or barrier semaphores. Data moves between devices by JAX's collectives and lax.ppermute only.
A program may use at most 128 MiB of HBM per device.

```python
import math
import jax
import jax.numpy as jnp
from jax import lax

D = 7168
HEADS = 128
KV_RANK = 512
ROPE = 64
NOPE = 128
VDIM = 128
Q_RANK = 1536
HALF = 64
GROUP = 2048
PREFIX = 3072


def draw_positions(key, part):
    key = jax.random.fold_in(key, 11)
    order = jax.random.permutation(key, GROUP // HALF)
    spread = order[:, None] * HALF + jnp.arange(HALF)[None, :]
    return spread.reshape(GROUP).astype(jnp.int32)


def draw_cache(key, part):
    key = jax.random.fold_in(key, 23)
    second = jax.random.fold_in(key, 1)
    width = KV_RANK + ROPE
    values = jax.random.normal(second, (PREFIX, width))
    return jnp.clip(values, -56.0, 56.0).astype(jnp.bfloat16)


def steps_of(stream_key, dims, shards, least, top_value):
    def one(dim, shards_of):
        steps = jax.random.uniform(jax.random.fold_in(jax.random.fold_in(stream_key, 6), dim), (shards_of,), jnp.float32, least / len(shards), top_value / len(shards))
        return jnp.repeat(jnp.exp(steps), dims[dim] // shards_of).reshape((-1,) + (1,) * (len(dims) - dim - 1))

    gain = one(*shards[0])
    for cut in shards[1:]:
        gain = gain * one(*cut)
    return gain


def centred(rng, shape, scale, limit, pieces=(), kind=jnp.bfloat16):
    result = scale * jax.random.normal(rng, shape, jnp.float32)
    if pieces:
        result = result * steps_of(rng, shape, pieces, -0.22, 0.18)
    return jnp.clip(result, -limit, limit).astype(kind)


def setup_inputs(seed: int = 0) -> dict:
    seeds = jax.random.split(jax.random.key(seed), 10)
    q_latent = centred(seeds[0], (GROUP, Q_RANK), 1.0, 6.0, ((0, 16),))
    kv_new = centred(seeds[1], (GROUP, KV_RANK + ROPE), 1.0, 6.0, ((0, 16),))
    cache = draw_cache(jax.random.fold_in(seeds[9], 71), 0)
    latent_gain = jnp.clip(1.0 + 0.18 * jax.random.normal(seeds[3], (KV_RANK,), jnp.float32), 0.1, 1.9)
    positions = draw_positions(jax.random.fold_in(seeds[9], 71), 0)
    w_uq = centred(seeds[5], (Q_RANK, HEADS * (NOPE + ROPE)), Q_RANK ** -0.5, 0.15625, ((1, 16),))
    w_uk = centred(seeds[6], (HEADS, NOPE, KV_RANK), NOPE ** -0.5, 0.5, ((0, 16),))
    w_uv = centred(seeds[7], (HEADS, KV_RANK, VDIM), (KV_RANK // 16) ** -0.5, 1.0, ((0, 16),))
    w_out = centred(seeds[8], (HEADS * VDIM, D), (HEADS * VDIM // 16) ** -0.5, 0.1875, ((0, 16), (1, 16)))
    return dict(q_latent=q_latent, kv_new=kv_new, cache=cache, latent_gain=latent_gain, positions=positions, w_uq=w_uq, w_uk=w_uk, w_uv=w_uv, w_out=w_out)


def angles(place, width):
    index = jnp.arange(width // 2, dtype=jnp.float32)
    inv_freq = jnp.exp(index * (-2.0 * math.log(10000.0) / width))
    return place[:, None] * inv_freq[None, :]

def rotate(vector, angle):
    half = vector.shape[-1] // 2
    first = vector[..., :half]
    second = vector[..., half:]
    cosine = jnp.cos(angle)
    sine = jnp.sin(angle)
    return jnp.concatenate([first * cosine - second * sine, first * sine + second * cosine], axis=-1)

def new_latents(kv_new, latent_gain, angle):
    latent = kv_new[:, :KV_RANK].astype(jnp.float32)
    square = lax.optimization_barrier(jnp.mean(latent * latent, axis=-1, keepdims=True)) + 1e-06
    normed = latent / jnp.sqrt(square) * latent_gain[None, :]
    rotated = rotate(kv_new[:, KV_RANK:].astype(jnp.float32), angle)
    return jnp.concatenate([normed, rotated], axis=-1).astype(jnp.bfloat16)

def reference(q_latent, kv_new, cache, latent_gain, positions, w_uq, w_uk, w_uv, w_out):
    query = jnp.dot(q_latent, w_uq, preferred_element_type=jnp.float32).astype(jnp.bfloat16)
    query = query.reshape(GROUP, HEADS, NOPE + ROPE)
    absorbed = jnp.einsum('thn,hnc->thc', query[:, :, :NOPE].astype(jnp.float32), w_uk.astype(jnp.float32)).astype(jnp.bfloat16)
    place = (positions + PREFIX).astype(jnp.float32)
    angle = angles(place, ROPE)
    q_rot = rotate(query[:, :, NOPE:].astype(jnp.float32), angle[:, None, :]).astype(jnp.bfloat16)
    fresh = new_latents(kv_new, latent_gain, angle)
    keys = jnp.concatenate([cache, fresh], axis=0)
    key_place = jnp.concatenate([jnp.full((PREFIX,), -1, jnp.int32), positions.astype(jnp.int32)])
    visible = key_place[None, :] <= positions.astype(jnp.int32)[:, None]
    joined = jnp.swapaxes(jnp.concatenate([absorbed, q_rot], axis=-1), 0, 1)
    scale = (NOPE + ROPE) ** (-0.5)

    def one_head(q_head):
        scores = jnp.dot(q_head, keys.T, preferred_element_type=jnp.float32) * scale
        scores = jnp.where(visible, scores, -jnp.inf)
        top = lax.optimization_barrier(jnp.max(scores, axis=1, keepdims=True))
        weights = jnp.exp(scores - top)
        total = lax.optimization_barrier(jnp.sum(weights, axis=1, keepdims=True))
        mixed = jnp.dot(weights.astype(jnp.bfloat16), keys[:, :KV_RANK], preferred_element_type=jnp.float32)
        return (mixed / total).astype(jnp.bfloat16)
    latent_out = lax.map(one_head, joined)
    values = jnp.einsum('htc,hcv->thv', latent_out.astype(jnp.float32), w_uv.astype(jnp.float32)).astype(jnp.bfloat16)
    values = values.reshape(GROUP, HEADS * VDIM)
    return jnp.dot(values, w_out, preferred_element_type=jnp.float32).astype(jnp.bfloat16)
```

```python
import functools
import math

import jax
import jax.numpy as jnp
from jax import lax
from jax.experimental import pallas as pl
from jax.experimental.pallas import tpu as pltpu
from jax.sharding import PartitionSpec as P

KV_RANK = 512
ROPE = 64
NOPE = 128
VDIM = 128
RUN = 64
PREFIX = 3072
WIDE = 640
AXES = ("seq", "head")
BIG = -1e30
F32 = jnp.float32
BF16 = jnp.bfloat16


def place_of(i):
    s, h = divmod(i, 16)
    return s // 2, s % 2, h // 4, (h // 2) % 2, h % 2


def index_of(z, xh, y, xl, c):
    return (z * 2 + xh) * 16 + y * 4 + xl * 2 + c


def pairs(to):
    return [(i, index_of(*to(*place_of(i)))) for i in range(256)]


def shift_z(d):
    return pairs(lambda z, xh, y, xl, c: ((z + d) % 8, xh, y, xl, c))


def shift_y(d):
    return pairs(lambda z, xh, y, xl, c: (z, xh, (y + d) % 4, xl, c))


SWAP_CORE = pairs(lambda z, xh, y, xl, c: (z, xh, y, xl, 1 - c))
SWAP_XH = pairs(lambda z, xh, y, xl, c: (z, 1 - xh, y, xl, c))
SWAP_MIRROR = pairs(lambda z, xh, y, xl, c: (z, 1 - xh, y, 1 - xl, c))

ORDER = (0, 1, -1, 2, -2, 3, -3, 4)


def final_pairs(same):
    def to(z, xh, y, xl, c):
        piece = 2 * y + (xl if same else 1 - xl)
        return (z + ORDER[piece]) % 8, xh, z >> 1, z & 1, c

    return pairs(to)


def permute(x, perm):
    return lax.ppermute(x, AXES, perm)


def angles(place, width):
    index = jnp.arange(width // 2, dtype=F32)
    inv_freq = jnp.exp(index * (-2.0 * math.log(10000.0) / width))
    return place[:, None] * inv_freq[None, :]


def query_kernel(lat_ref, wq_ref, wk_ref, cos_ref, sin_ref, mask_ref, out_ref):
    scale = (NOPE + ROPE) ** (-0.5) * math.log2(math.e)
    query = jnp.dot(lat_ref[...], wq_ref[...], preferred_element_type=F32).astype(BF16)
    for i in range(2):
        part = query[:, i * 192 : (i + 1) * 192]
        absorbed = jnp.dot(part[:, :NOPE], wk_ref[i], preferred_element_type=F32)
        out_ref[i, :, :KV_RANK] = (absorbed * scale).astype(BF16)
        rope = part[:, NOPE:].astype(F32)
        swapped = jnp.concatenate([rope[:, ROPE // 2 :], rope[:, : ROPE // 2]], axis=1)
        rotated = rope * cos_ref[...] + swapped * sin_ref[...]
        out_ref[i, :, KV_RANK:] = jnp.concatenate(
            [(rotated * scale).astype(BF16), mask_ref[...]], axis=1
        )


def queries(lat, w_uq, w_uk, cosine, sine, mask):
    rows = lat.shape[0]
    heads = w_uk.shape[0]
    whole = lambda i: (0, 0)
    return pl.pallas_call(
        query_kernel,
        grid=(heads // 2,),
        in_specs=[
            pl.BlockSpec(lat.shape, whole),
            pl.BlockSpec((w_uq.shape[0], 384), lambda i: (0, i)),
            pl.BlockSpec((2, NOPE, KV_RANK), lambda i: (i, 0, 0)),
            pl.BlockSpec(cosine.shape, whole),
            pl.BlockSpec(sine.shape, whole),
            pl.BlockSpec(mask.shape, whole),
        ],
        out_specs=pl.BlockSpec((2, rows, WIDE), lambda i: (i, 0, 0)),
        out_shape=jax.ShapeDtypeStruct((heads, rows, WIDE), BF16),
        compiler_params=pltpu.CompilerParams(vmem_limit_bytes=32 * 2**20),
        cost_estimate=pl.CostEstimate(
            flops=2 * rows * heads * (1536 * 192 + 128 * 512),
            bytes_accessed=10 * 2**20,
            transcendentals=0,
        ),
    )(lat, w_uq, w_uk, cosine, sine, mask)


def attend_kernel(q_ref, ka_ref, kb_ref, bias_ref, wv_ref, out_ref, top_ref, total_ref, s_ref):
    nt = (((1,), (1,)), ((), ()))
    group, rows = q_ref.shape[0], q_ref.shape[1]
    half = ka_ref.shape[0]
    for i in range(group):
        q = q_ref[i]
        tops = []
        for part, keys in enumerate((ka_ref, kb_ref)):
            for j in range(half // 256):
                scores = lax.dot_general(
                    q, keys[j * 256 : (j + 1) * 256, :], nt, preferred_element_type=F32
                )
                if j == 0:
                    scores = scores + bias_ref[part]
                at = part * half + j * 256
                s_ref[:, at : at + 256] = scores
                tops.append(jnp.maximum(scores[:, :128], scores[:, 128:]))
        top = functools.reduce(jnp.maximum, tops)
        top = jnp.max(top, axis=1, keepdims=True)
        total = jnp.zeros((rows, 128), F32)
        accum = jnp.zeros((rows, KV_RANK), F32)
        for part, keys in enumerate((ka_ref, kb_ref)):
            for j in range(half // 256):
                at = part * half + j * 256
                weights = jnp.exp2(s_ref[:, at : at + 256] - top)
                total = total + (weights[:, :128] + weights[:, 128:])
                accum = accum + jnp.dot(
                    weights.astype(BF16),
                    keys[j * 256 : (j + 1) * 256, :KV_RANK],
                    preferred_element_type=F32,
                )
        total = jnp.sum(total, axis=1, keepdims=True)
        latent = (accum / total).astype(BF16)
        out_ref[:, i * VDIM : (i + 1) * VDIM] = jnp.dot(
            latent, wv_ref[i], preferred_element_type=F32
        ).astype(BF16)
        top_ref[i] = jnp.broadcast_to(top, (rows, 128))
        total_ref[i] = jnp.broadcast_to(total, (rows, 128))


def attend(q, ka, kb, bias, w_uv):
    heads, rows, _ = q.shape
    half = ka.shape[0]
    group = 2
    stat = jax.ShapeDtypeStruct((heads, rows, 128), F32)
    stat_spec = pl.BlockSpec((group, rows, 128), lambda i: (i, 0, 0))
    return pl.pallas_call(
        attend_kernel,
        grid=(heads // group,),
        in_specs=[
            pl.BlockSpec((group, rows, WIDE), lambda i: (i, 0, 0)),
            pl.BlockSpec(ka.shape, lambda i: (0, 0)),
            pl.BlockSpec(kb.shape, lambda i: (0, 0)),
            pl.BlockSpec(bias.shape, lambda i: (0, 0, 0)),
            pl.BlockSpec((group, KV_RANK, VDIM), lambda i: (i, 0, 0)),
        ],
        out_specs=[
            pl.BlockSpec((rows, group * VDIM), lambda i: (0, i)),
            stat_spec,
            stat_spec,
        ],
        out_shape=[jax.ShapeDtypeStruct((rows, heads * VDIM), BF16), stat, stat],
        scratch_shapes=[pltpu.VMEM((rows, 2 * half), F32)],
        compiler_params=pltpu.CompilerParams(vmem_limit_bytes=48 * 2**20),
        cost_estimate=pl.CostEstimate(
            flops=2 * rows * heads * 2 * half * (WIDE + KV_RANK),
            bytes_accessed=10 * 2**20,
            transcendentals=rows * heads * 2 * half,
        ),
    )(q, ka, kb, bias, w_uv)


def ring(own):
    rows = own.shape[0]
    up, down = own, own
    got = [own]
    for _ in range(3):
        up = permute(up, shift_z(1))
        down = permute(down, shift_z(-1))
        got += [down, up]
    far_up = permute(up[: rows // 2], shift_z(1))
    far_down = permute(down[rows // 2 :], shift_z(-1))
    return got + [far_up, far_down]


def per_device(q_latent, kv_new, cache, latent_gain, positions, w_uq, w_uk, w_uv, w_out):
    rows = q_latent.shape[0]
    heads = w_uk.shape[0]
    head_index = lax.axis_index("head")
    seq_index = lax.axis_index("seq")
    core = head_index % 2
    x_hi = seq_index % 2

    run = positions // RUN
    lane = jnp.arange(128)[None, :]
    marks = jnp.where(
        lane == 0, run[:, None], jnp.where(lane == 1, (positions % RUN)[:, None], 0)
    ).astype(BF16)
    sent = jnp.concatenate([q_latent, marks], axis=1)
    other = permute(sent, SWAP_MIRROR)
    w_other = permute(w_out, SWAP_XH)

    place = (positions + PREFIX).astype(F32)
    angle = angles(place, ROPE)
    cos_own, sin_own = jnp.cos(angle), jnp.sin(angle)
    latent = kv_new[:, :KV_RANK].astype(F32)
    square = jnp.mean(latent * latent, axis=-1, keepdims=True) + 1e-06
    normed = latent / jnp.sqrt(square) * latent_gain[None, :]
    rope = kv_new[:, KV_RANK:].astype(F32)
    first, second = rope[:, : ROPE // 2], rope[:, ROPE // 2 :]
    one_hot = (run[:, None] == jnp.arange(WIDE - KV_RANK - ROPE)[None, :]).astype(F32)
    fresh = jnp.concatenate(
        [
            normed,
            first * cos_own - second * sin_own,
            first * sin_own + second * cos_own,
            one_hot,
        ],
        axis=1,
    ).astype(BF16)
    old = jnp.pad(cache, ((0, 0), (0, WIDE - KV_RANK - ROPE)))
    old_rows = old.shape[0] // 2
    own = jnp.concatenate(
        [
            lax.dynamic_slice_in_dim(old, core * old_rows, old_rows, 0),
            lax.dynamic_slice_in_dim(fresh, core * RUN, RUN, 0),
        ],
        axis=0,
    )
    keys = jnp.concatenate(ring(own), axis=0)
    keys_other = permute(keys, SWAP_CORE)

    other_marks = other[:, 1536:1538].astype(jnp.int32)
    other_run = other_marks[:, 0]
    other_positions = other_run * RUN + other_marks[:, 1]
    other_angle = angles((other_positions + PREFIX).astype(F32), ROPE)
    cos = jnp.concatenate([cos_own, jnp.cos(other_angle)], axis=0)
    sin = jnp.concatenate([sin_own, jnp.sin(other_angle)], axis=0)
    both_run = jnp.concatenate([run, other_run], axis=0)
    mask = jnp.where(jnp.arange(WIDE - KV_RANK - ROPE)[None, :] > both_run[:, None], BIG, 0.0)
    lat = jnp.concatenate([q_latent, other[:, :1536]], axis=0)
    q = queries(
        lat,
        w_uq,
        w_uk,
        jnp.concatenate([cos, cos], axis=1),
        jnp.concatenate([-sin, sin], axis=1),
        mask.astype(BF16),
    )

    token = jnp.arange(2 * rows)[None, :, None]
    slot = jnp.arange(256)[None, None, :]
    of_core = jnp.stack([core, 1 - core])[:, None, None]
    hidden = (
        (token < rows)
        & (token // RUN == of_core)
        & (slot >= old_rows)
        & (slot < old_rows + RUN)
        & (slot - old_rows > token % RUN)
    )
    bias = jnp.where(hidden, BIG, 0.0).astype(F32)
    part, top, total = attend(q, keys, keys_other, bias, w_uv)

    lse = (top + jnp.log2(total))[:, :, 0].T
    lse_high = lse.astype(BF16)
    rest = lse - lse_high.astype(F32)
    lse_mid = rest.astype(BF16)
    lse_low = (rest - lse_mid.astype(F32)).astype(BF16)
    packed = jnp.concatenate(
        [
            part[rows:],
            lse_high[rows:],
            lse_mid[rows:],
            lse_low[rows:],
            jnp.zeros((rows, 128 - 3 * heads), BF16),
        ],
        axis=1,
    )
    came = permute(packed, SWAP_XH)
    wide = heads * VDIM
    came_lse = sum(
        came[:, wide + i * heads : wide + (i + 1) * heads].astype(F32) for i in range(3)
    )
    own_lse = lse[:rows]
    best = jnp.maximum(own_lse, came_lse)
    own_weight = jnp.exp2(own_lse - best)
    came_weight = jnp.exp2(came_lse - best)
    both = own_weight + came_weight
    spread = lambda w: jnp.repeat(w / both, VDIM, axis=1)
    values = (
        part[:rows].astype(F32) * spread(own_weight)
        + came[:, :wide].astype(F32) * spread(came_weight)
    ).astype(BF16)

    same = x_hi == core
    w_keep = jnp.where(same, w_out, w_other)
    w_send = jnp.where(same, w_other, w_out)
    values = jnp.concatenate(ring(values), axis=0)
    send = jnp.dot(values, w_send, preferred_element_type=F32).astype(BF16)
    came = permute(send, SWAP_CORE)
    keep = jnp.dot(values, w_keep, preferred_element_type=F32)
    summed = (keep + came.astype(F32)).astype(BF16)

    y = head_index // 4
    x_lo = (head_index // 2) % 2
    take = lambda at: lax.dynamic_slice_in_dim(summed, at * 2 * rows, 2 * rows, 0)
    parts = [permute(take((y + d) % 4), shift_y(d)) for d in (1, 3, 2)]
    mine = take(y).astype(F32) + sum(p.astype(F32) for p in parts)
    mine = mine.astype(BF16)
    straight = permute(lax.dynamic_slice_in_dim(mine, x_lo * rows, rows, 0), final_pairs(True))
    crossed = permute(
        lax.dynamic_slice_in_dim(mine, (1 - x_lo) * rows, rows, 0), final_pairs(False)
    )
    return (straight.astype(F32) + crossed.astype(F32)).astype(BF16)


def solution(mesh):
    placed = (
        P("seq", None),
        P("seq", None),
        P("seq", None),
        P(),
        P("seq"),
        P(None, "head"),
        P("head", None, None),
        P("head", None, None),
        P("head", "seq"),
    )
    return jax.shard_map(
        per_device, mesh=mesh, in_specs=placed, out_specs=P("seq", "head"), check_vma=False
    )
```

```python
import functools
import math

import jax
import jax.numpy as jnp
from jax import lax
from jax.experimental import pallas as pl
from jax.experimental.pallas import tpu as pltpu
from jax.sharding import PartitionSpec as P

KV_RANK = 512
ROPE = 64
NOPE = 128
VDIM = 128
RUN = 64
PREFIX = 3072
WIDE = 640
CHUNK = 512
AXES = ("seq", "head")
BIG = -1e30
F32 = jnp.float32
BF16 = jnp.bfloat16


def place_of(i):
    s, h = divmod(i, 16)
    return s // 2, s % 2, h // 4, (h // 2) % 2, h % 2


def index_of(z, xh, y, xl, c):
    return (z * 2 + xh) * 16 + y * 4 + xl * 2 + c


def pairs(to):
    return [(i, index_of(*to(*place_of(i)))) for i in range(256)]


def next_to(i, size):
    return (i + 1 if i % 2 else i - 1) % size


SWAP_CORE = pairs(lambda z, xh, y, xl, c: (z, xh, y, xl, 1 - c))
SWAP_XH = pairs(lambda z, xh, y, xl, c: (z, 1 - xh, y, xl, c))
SWAP_MIRROR = pairs(lambda z, xh, y, xl, c: (z, 1 - xh, y, 1 - xl, c))
SWAP_Z = (
    pairs(lambda z, xh, y, xl, c: (z ^ 1, xh, y, xl, c)),
    pairs(lambda z, xh, y, xl, c: (next_to(z, 8), xh, y, xl, c)),
)
SWAP_Y = (
    pairs(lambda z, xh, y, xl, c: (z, xh, y ^ 1, xl, c)),
    pairs(lambda z, xh, y, xl, c: (z, xh, next_to(y, 4), xl, c)),
    pairs(lambda z, xh, y, xl, c: (z, xh, y ^ 2, xl, c)),
)


def final_pairs(same):
    def to(z, xh, y, xl, c):
        return 2 * y + (xl if same else 1 - xl), xh, z >> 1, z & 1, c

    return pairs(to)


def permute(x, perm):
    return lax.ppermute(x, AXES, perm)


def angles(place, width):
    index = jnp.arange(width // 2, dtype=F32)
    inv_freq = jnp.exp(index * (-2.0 * math.log(10000.0) / width))
    return place[:, None] * inv_freq[None, :]


def query_kernel(lat_ref, wq_ref, wk_ref, cos_ref, sin_ref, mask_ref, out_ref):
    scale = (NOPE + ROPE) ** (-0.5) * math.log2(math.e)
    query = jnp.dot(lat_ref[...], wq_ref[...], preferred_element_type=F32).astype(BF16)
    for i in range(2):
        part = query[:, i * 192 : (i + 1) * 192]
        absorbed = jnp.dot(part[:, :NOPE], wk_ref[i], preferred_element_type=F32)
        out_ref[i, :, :KV_RANK] = (absorbed * scale).astype(BF16)
        rope = part[:, NOPE:].astype(F32)
        swapped = jnp.concatenate([rope[:, ROPE // 2 :], rope[:, : ROPE // 2]], axis=1)
        rotated = rope * cos_ref[...] + swapped * sin_ref[...]
        out_ref[i, :, KV_RANK:] = jnp.concatenate(
            [(rotated * scale).astype(BF16), mask_ref[...]], axis=1
        )


def queries(lat, w_uq, w_uk, cosine, sine, mask):
    rows = lat.shape[0]
    heads = w_uk.shape[0]
    whole = lambda i: (0, 0)
    return pl.pallas_call(
        query_kernel,
        grid=(heads // 2,),
        in_specs=[
            pl.BlockSpec(lat.shape, whole),
            pl.BlockSpec((w_uq.shape[0], 384), lambda i: (0, i)),
            pl.BlockSpec((2, NOPE, KV_RANK), lambda i: (i, 0, 0)),
            pl.BlockSpec(cosine.shape, whole),
            pl.BlockSpec(sine.shape, whole),
            pl.BlockSpec(mask.shape, whole),
        ],
        out_specs=pl.BlockSpec((2, rows, WIDE), lambda i: (i, 0, 0)),
        out_shape=jax.ShapeDtypeStruct((heads, rows, WIDE), BF16),
        compiler_params=pltpu.CompilerParams(vmem_limit_bytes=32 * 2**20),
        cost_estimate=pl.CostEstimate(
            flops=rows * heads * (1536 * 192 + 128 * 512) // 4,
            bytes_accessed=2**20,
            transcendentals=0,
        ),
    )(lat, w_uq, w_uk, cosine, sine, mask)


def lanes(x, fill):
    width = x.shape[1]
    blocks = [x[:, at : min(at + 128, width)] for at in range(0, width, 128)]
    short = 128 - blocks[-1].shape[1]
    if short:
        rest = jnp.full((x.shape[0], short), fill, x.dtype)
        blocks[-1] = jnp.concatenate([blocks[-1], rest], axis=1)
    return blocks


def attend_kernel(stack, kind, *refs):
    q_ref, k_ref, wv_ref = refs[:3]
    refs = list(refs[3:])
    bias_ref = refs.pop(0) if kind == "first" else None
    before = [(refs.pop(0), refs.pop(0)) for _ in range(2)] if kind in ("own", "packed") else []
    top_ref = refs.pop()
    s_ref = refs.pop()
    out_ref = refs[0]
    heads, rows, _ = q_ref.shape
    count = k_ref.shape[0]
    groups = heads // stack
    many = stack * rows
    cuts = [(at, min(at + CHUNK, count)) for at in range(0, count, CHUNK)]
    nt = (((1,), (1,)), ((), ()))
    lane = lax.broadcasted_iota(jnp.int32, (rows, 128), 1)

    def score(group, slot, cut):
        start, end = cut
        q = q_ref[group * stack : (group + 1) * stack].reshape(many, WIDE)
        scores = lax.dot_general(q, k_ref[start:end, :], nt, preferred_element_type=F32)
        if bias_ref is not None and start == 0:
            bias = jnp.concatenate([bias_ref[...]] * stack, axis=0)
            scores = jnp.concatenate([scores[:, :128] + bias, scores[:, 128:]], axis=1)
        s_ref[slot, :, start:end] = scores
        return functools.reduce(jnp.maximum, lanes(scores, BIG))

    def finish(group, latent, lse, kept):
        for i in range(stack):
            part = slice(i * rows, (i + 1) * rows)
            head = group * stack + i
            at = slice(head * VDIM, (head + 1) * VDIM)
            value = jnp.dot(latent[part], wv_ref[head], preferred_element_type=F32)
            level = lse[part]
            if before:
                values, levels = [value], [level]
                for value_ref, level_ref in before:
                    values.append(value_ref[:, at])
                    chosen = jnp.where(lane == head, level_ref[...], 0.0)
                    levels.append(jnp.sum(chosen, axis=1, keepdims=True))
                best = functools.reduce(jnp.maximum, levels)
                shares = [jnp.exp2(x - best) for x in levels]
                whole = functools.reduce(jnp.add, shares)
                value = functools.reduce(jnp.add, [v * w for v, w in zip(values, shares)])
                value = value / whole
                level = best + jnp.log2(whole)
            out_ref[:, at] = value.astype(out_ref.dtype)
            kept = jnp.where(lane % 8 == head, level, kept)
        return kept

    def turn(group, kept, more):
        slot, other = group % 2, (group + 1) % 2
        top = jnp.max(top_ref[...], axis=1, keepdims=True)
        total = jnp.zeros((many, 128), F32)
        accum = None
        tops = []
        for start, end in cuts:
            weights = jnp.exp2(s_ref[slot, :, start:end] - top)
            for block in lanes(weights, 0.0):
                total = total + block
            mixed = jnp.dot(
                weights.astype(BF16), k_ref[start:end, :KV_RANK], preferred_element_type=F32
            )
            accum = mixed if accum is None else accum + mixed
            if more:
                tops.append(score(group + 1, other, (start, end)))
        if more:
            top_ref[...] = functools.reduce(jnp.maximum, tops)
        total = jnp.sum(total, axis=1, keepdims=True)
        return finish(group, (accum / total).astype(BF16), top + jnp.log2(total), kept)

    top_ref[...] = functools.reduce(jnp.maximum, [score(0, 0, cut) for cut in cuts])
    kept = jnp.zeros((rows, 128), F32)
    for group in range(groups):
        kept = turn(group, kept, group + 1 < groups)
    if kind != "packed":
        refs[1][...] = kept
        return
    high = kept.astype(BF16)
    rest = kept - high.astype(F32)
    mid = rest.astype(BF16)
    low = (rest - mid.astype(F32)).astype(BF16)
    out_ref[:, heads * VDIM :] = jnp.where(lane < 8, high, jnp.where(lane < 16, mid, low))


def attend(q, keys, w_uv, kind, bias=None, before=()):
    heads, rows, _ = q.shape
    count = keys.shape[0]
    stack = 4
    operands = [q, keys, w_uv]
    if bias is not None:
        operands.append(bias)
    for pair in before:
        operands += pair
    wide = heads * VDIM
    out_shape = [jax.ShapeDtypeStruct((rows, wide), F32), jax.ShapeDtypeStruct((rows, 128), F32)]
    if kind == "packed":
        out_shape = [jax.ShapeDtypeStruct((rows, wide + 128), BF16)]
    spec = pl.BlockSpec(memory_space=pltpu.VMEM)
    return pl.pallas_call(
        functools.partial(attend_kernel, stack, kind),
        in_specs=[spec] * len(operands),
        out_specs=[spec] * len(out_shape),
        out_shape=out_shape,
        scratch_shapes=[
            pltpu.VMEM((2, stack * rows, -(-count // 128) * 128), F32),
            pltpu.VMEM((stack * rows, 128), F32),
        ],
        compiler_params=pltpu.CompilerParams(vmem_limit_bytes=24 * 2**20),
        cost_estimate=pl.CostEstimate(
            flops=rows * heads * count * (WIDE + KV_RANK) // 8,
            bytes_accessed=2**19,
            transcendentals=0,
        ),
    )(*operands)


def prepare_kernel(kv_ref, cache_ref, gain_ref, cos_ref, sin_ref, run_ref, own_ref, keys_ref):
    core = lax.axis_index("head") % 2
    rows = kv_ref.shape[0]
    half = cache_ref.shape[0] // 2
    spare = WIDE - KV_RANK - ROPE
    latent = kv_ref[:, :KV_RANK].astype(F32)
    square = jnp.sum(latent * latent, axis=1, keepdims=True) / KV_RANK + 1e-06
    normed = latent / jnp.sqrt(square) * gain_ref[...]
    rope = kv_ref[:, KV_RANK:].astype(F32)
    swapped = jnp.concatenate([rope[:, ROPE // 2 :], rope[:, : ROPE // 2]], axis=1)
    rotated = rope * cos_ref[...] + swapped * sin_ref[...]
    slot = lax.broadcasted_iota(jnp.int32, (rows, spare), 1)
    one_hot = (run_ref[...] == slot).astype(F32)
    keys_ref[:rows, :KV_RANK] = normed.astype(BF16)
    keys_ref[:rows, KV_RANK:] = jnp.concatenate([rotated, one_hot], axis=1).astype(BF16)
    keys_ref[rows:, :KV_RANK] = cache_ref[:, :KV_RANK]
    keys_ref[rows:, KV_RANK:] = jnp.concatenate(
        [cache_ref[:, KV_RANK:], jnp.zeros((2 * half, spare), BF16)], axis=1
    )
    for i in range(2):

        @pl.when(core == i)
        def _():
            own_ref[:half] = keys_ref[rows + i * half : rows + (i + 1) * half]
            own_ref[half:] = keys_ref[i * RUN : (i + 1) * RUN]


def prepare(kv_new, cache, gain, cosine, sine, run):
    rows, old = kv_new.shape[0], cache.shape[0]
    spec = pl.BlockSpec(memory_space=pltpu.VMEM)
    return pl.pallas_call(
        prepare_kernel,
        in_specs=[spec] * 6,
        out_specs=[spec] * 2,
        out_shape=[
            jax.ShapeDtypeStruct(((rows + old) // 2, WIDE), BF16),
            jax.ShapeDtypeStruct((rows + old, WIDE), BF16),
        ],
        compiler_params=pltpu.CompilerParams(vmem_limit_bytes=16 * 2**20),
    )(kv_new, cache, gain, cosine, sine, run)


def tie(*arrays):
    return lax.optimization_barrier(arrays)


def step_z(a, b):
    return permute(b, SWAP_Z[0]), permute(a, SWAP_Z[1])


def both_cores(*pieces):
    mine = jnp.concatenate(pieces, axis=0)
    return mine, permute(mine, SWAP_CORE)


def turning(place):
    angle = angles(place.astype(F32), ROPE)
    cosine, sine = jnp.cos(angle), jnp.sin(angle)
    return jnp.concatenate([cosine, cosine], axis=1), jnp.concatenate([-sine, sine], axis=1)


def per_device(q_latent, kv_new, cache, latent_gain, positions, w_uq, w_uk, w_uv, w_out):
    rows = q_latent.shape[0]
    heads = w_uk.shape[0]
    head_index = lax.axis_index("head")
    seq_index = lax.axis_index("seq")
    core = head_index % 2
    x_hi = seq_index % 2
    spare = WIDE - KV_RANK - ROPE

    run = positions // RUN
    lane = jnp.arange(128)[None, :]
    marks = jnp.where(
        lane == 0, run[:, None], jnp.where(lane == 1, (positions % RUN)[:, None], 0)
    ).astype(BF16)
    other = permute(jnp.concatenate([q_latent, marks], axis=1), SWAP_MIRROR)

    cos_own, sin_own = turning(positions + PREFIX)
    own, keys_0 = prepare(
        kv_new, cache, latent_gain[None, :], cos_own, sin_own, run[:, None]
    )
    a_1, b_1 = step_z(own, own)
    mask = lambda r: jnp.where(jnp.arange(spare)[None, :] > r[:, None], BIG, 0.0).astype(BF16)
    q_own = queries(q_latent, w_uq, w_uk, cos_own, sin_own, mask(run))
    q_own, a_1, b_1 = tie(q_own, a_1, b_1)

    a_2, b_2 = step_z(a_1, b_1)
    mine_1, theirs_1 = both_cores(a_1, b_1)
    keys_1 = jnp.concatenate([keys_0, mine_1, theirs_1], axis=0)
    token = jnp.arange(rows)[:, None]
    hidden = (token // RUN == lane // RUN) & (lane % RUN > token % RUN)
    bias = jnp.where(hidden, BIG, 0.0).astype(F32)
    own_1 = attend(q_own, keys_1, w_uv, "first", bias=bias)
    own_1, a_2, b_2, other = tie(own_1, a_2, b_2, other)

    a_3, b_3 = step_z(a_2, b_2)
    mine_2, theirs_2 = both_cores(a_2, b_2)
    w_half = w_out.shape[0] // 2
    w_sent, other = tie(w_out[:w_half], other)
    w_first = permute(w_sent, SWAP_XH)
    other_marks = other[:, 1536:1538].astype(jnp.int32)
    other_run = other_marks[:, 0]
    cos_other, sin_other = turning(other_run * RUN + other_marks[:, 1] + PREFIX)
    q_other = queries(
        other[:, :1536], w_uq, w_uk, cos_other, sin_other, mask(other_run)
    )
    other_1 = attend(q_other, keys_1, w_uv, "next")
    other_1, a_3, b_3 = tie(other_1, a_3, b_3)

    half = a_3.shape[0] // 2
    a_4, b_4 = step_z(a_3[half:], b_3[:half])
    keys_2 = jnp.concatenate([mine_2, theirs_2], axis=0)
    other_2 = attend(q_other, keys_2, w_uv, "next")
    own_2 = attend(q_own, keys_2, w_uv, "next")
    own_2, other_2, a_4, b_4, w_first = tie(own_2, other_2, a_4, b_4, w_first)
    mine_3, theirs_3 = both_cores(a_3, b_3, a_4, b_4)
    keys_3 = jnp.concatenate([mine_3, theirs_3], axis=0)
    (packed,) = attend(q_other, keys_3, w_uv, "packed", before=(other_1, other_2))
    came = permute(packed, SWAP_XH)
    q_own, packed = tie(q_own, packed)
    merged, own_lse = attend(q_own, keys_3, w_uv, "own", before=(own_1, own_2))

    wide = heads * VDIM
    came_lse = sum(
        came[:, wide + i * heads : wide + (i + 1) * heads].astype(F32) for i in range(3)
    )
    own_lse = own_lse[:, :heads]
    best = jnp.maximum(own_lse, came_lse)
    own_weight = jnp.exp2(own_lse - best)
    came_weight = jnp.exp2(came_lse - best)
    both = own_weight + came_weight
    spread = lambda w: jnp.repeat(w / both, VDIM, axis=1)
    values = (
        merged * spread(own_weight) + came[:, :wide].astype(F32) * spread(came_weight)
    ).astype(BF16)

    z = seq_index // 2
    y = head_index // 4
    x_lo = (head_index // 2) % 2
    odd = z % 2

    def project(*blocks):
        block = jnp.concatenate(blocks, axis=0)
        send = jnp.dot(block, w_send, preferred_element_type=F32).astype(BF16)
        came = permute(send, SWAP_CORE)
        keep = jnp.dot(block, w_keep, preferred_element_type=F32)
        return (keep + came.astype(F32)).astype(BF16)

    def across(summed, swapped):
        def take(of):
            away = (of - z // 2) % 4
            side = jnp.where((away == 1) == (swapped == 1), 2, 1)
            at = jnp.where(away == 0, 0, jnp.where(away == 2, 3, side))
            return lax.dynamic_slice_in_dim(summed, at * rows, rows, 0)

        others = (y ^ 1, (y + jnp.where(y % 2 == 1, 1, 3)) % 4, y ^ 2)
        parts = [permute(take(of), swap) for of, swap in zip(others, SWAP_Y)]
        mine = take(y).astype(F32) + sum(p.astype(F32) for p in parts)
        return mine.astype(BF16)

    w_sent, values = tie(w_out[w_half:], values)
    w_second = permute(w_sent, SWAP_XH)
    a_1, b_1 = step_z(values, values)
    a_2, b_2 = step_z(a_1, b_1)
    a_2, b_2, w_second = tie(a_2, b_2, w_second)
    a_3, b_3 = step_z(a_2, b_2)
    same = x_hi == core
    w_other = jnp.concatenate([w_first, w_second], axis=0)
    w_keep = jnp.where(same, w_out, w_other)
    w_send = jnp.where(same, w_other, w_out)
    half = rows // 2
    a_4, b_4 = step_z(a_3[half:], b_3[:half])
    odd_wave = across(project(a_1, b_1, a_3, b_3), 1 - odd)
    even_wave = across(project(values, a_2, b_2, a_4, b_4), odd)

    even = x_lo == odd
    straight = permute(jnp.where(even, even_wave, odd_wave), final_pairs(True))
    crossed = permute(jnp.where(even, odd_wave, even_wave), final_pairs(False))
    return (straight.astype(F32) + crossed.astype(F32)).astype(BF16)


def solution(mesh):
    placed = (
        P("seq", None),
        P("seq", None),
        P("seq", None),
        P(),
        P("seq"),
        P(None, "head"),
        P("head", None, None),
        P("head", None, None),
        P("head", "seq"),
    )
    return jax.shard_map(
        per_device, mesh=mesh, in_specs=placed, out_specs=P("seq", "head"), check_vma=False
    )
```

```python
import functools
import math

import jax
import jax.numpy as jnp
from jax import lax
from jax.experimental import pallas as pl
from jax.experimental.pallas import tpu as pltpu
from jax.sharding import PartitionSpec as P

KV_RANK = 512
ROPE = 64
NOPE = 128
VDIM = 128
RUN = 64
PREFIX = 3072
WIDE = 640
CHUNK = 512
AXES = ("seq", "head")
BIG = -1e30
F32 = jnp.float32
BF16 = jnp.bfloat16


def place_of(i):
    s, h = divmod(i, 16)
    return s // 2, s % 2, h // 4, (h // 2) % 2, h % 2


def index_of(z, xh, y, xl, c):
    return (z * 2 + xh) * 16 + y * 4 + xl * 2 + c


def pairs(to):
    moves = [(i, to(*place_of(i))) for i in range(256)]
    return [(i, index_of(*place)) for i, place in moves if place]


def next_to(i, size):
    return (i + 1 if i % 2 else i - 1) % size


SWAP_CORE = pairs(lambda z, xh, y, xl, c: (z, xh, y, xl, 1 - c))
SWAP_XH = pairs(lambda z, xh, y, xl, c: (z, 1 - xh, y, xl, c))
SWAP_MIRROR = pairs(lambda z, xh, y, xl, c: (z, 1 - xh, y, 1 - xl, c))
SWAP_Z = (
    pairs(lambda z, xh, y, xl, c: (z ^ 1, xh, y, xl, c)),
    pairs(lambda z, xh, y, xl, c: (next_to(z, 8), xh, y, xl, c)),
)
SWAP_Y = (
    pairs(lambda z, xh, y, xl, c: (z, xh, y ^ 1, xl, c)),
    pairs(lambda z, xh, y, xl, c: (z, xh, next_to(y, 4), xl, c)),
    pairs(lambda z, xh, y, xl, c: (z, xh, y ^ 2, xl, c)),
)


SWAP_XL = pairs(lambda z, xh, y, xl, c: (z, xh, y, 1 - xl, c))
TO_PLACE = pairs(lambda z, xh, y, xl, c: (2 * y + xl, xh, z >> 1, z & 1, c))


def permute(x, perm):
    return lax.ppermute(x, AXES, perm)


def angles(place, width):
    index = jnp.arange(width // 2, dtype=F32)
    inv_freq = jnp.exp(index * (-2.0 * math.log(10000.0) / width))
    return place[:, None] * inv_freq[None, :]


def query_kernel(lat_ref, wq_ref, wk_ref, cos_ref, sin_ref, mask_ref, out_ref):
    scale = (NOPE + ROPE) ** (-0.5) * math.log2(math.e)
    query = jnp.dot(lat_ref[...], wq_ref[...], preferred_element_type=F32).astype(BF16)
    for i in range(2):
        part = query[:, i * 192 : (i + 1) * 192]
        absorbed = jnp.dot(part[:, :NOPE], wk_ref[i], preferred_element_type=F32)
        out_ref[i, :, :KV_RANK] = (absorbed * scale).astype(BF16)
        rope = part[:, NOPE:].astype(F32)
        swapped = jnp.concatenate([rope[:, ROPE // 2 :], rope[:, : ROPE // 2]], axis=1)
        rotated = rope * cos_ref[...] + swapped * sin_ref[...]
        out_ref[i, :, KV_RANK:] = jnp.concatenate(
            [(rotated * scale).astype(BF16), mask_ref[...]], axis=1
        )


def queries(lat, w_uq, w_uk, cosine, sine, mask):
    rows = lat.shape[0]
    heads = w_uk.shape[0]
    whole = lambda i: (0, 0)
    return pl.pallas_call(
        query_kernel,
        grid=(heads // 2,),
        in_specs=[
            pl.BlockSpec(lat.shape, whole),
            pl.BlockSpec((w_uq.shape[0], 384), lambda i: (0, i)),
            pl.BlockSpec((2, NOPE, KV_RANK), lambda i: (i, 0, 0)),
            pl.BlockSpec(cosine.shape, whole),
            pl.BlockSpec(sine.shape, whole),
            pl.BlockSpec(mask.shape, whole),
        ],
        out_specs=pl.BlockSpec((2, rows, WIDE), lambda i: (i, 0, 0)),
        out_shape=jax.ShapeDtypeStruct((heads, rows, WIDE), BF16),
        compiler_params=pltpu.CompilerParams(vmem_limit_bytes=32 * 2**20),
        cost_estimate=pl.CostEstimate(
            flops=rows * heads * (1536 * 192 + 128 * 512) // 4,
            bytes_accessed=2**20,
            transcendentals=0,
        ),
    )(lat, w_uq, w_uk, cosine, sine, mask)


def lanes(x, fill):
    width = x.shape[1]
    blocks = [x[:, at : min(at + 128, width)] for at in range(0, width, 128)]
    short = 128 - blocks[-1].shape[1]
    if short:
        rest = jnp.full((x.shape[0], short), fill, x.dtype)
        blocks[-1] = jnp.concatenate([blocks[-1], rest], axis=1)
    return blocks


def attend_kernel(stack, kind, *refs):
    q_ref, k_ref, wv_ref = refs[:3]
    refs = list(refs[3:])
    bias_ref = refs.pop(0) if kind == "first" else None
    before = [(refs.pop(0), refs.pop(0)) for _ in range(2)] if kind in ("own", "packed") else []
    top_ref = refs.pop()
    s_ref = refs.pop()
    out_ref = refs[0]
    heads, rows, _ = q_ref.shape
    count = k_ref.shape[0]
    groups = heads // stack
    many = stack * rows
    cuts = [(at, min(at + CHUNK, count)) for at in range(0, count, CHUNK)]
    nt = (((1,), (1,)), ((), ()))
    lane = lax.broadcasted_iota(jnp.int32, (rows, 128), 1)

    def score(group, slot, cut):
        start, end = cut
        q = q_ref[group * stack : (group + 1) * stack].reshape(many, WIDE)
        scores = lax.dot_general(q, k_ref[start:end, :], nt, preferred_element_type=F32)
        if bias_ref is not None and start == 0:
            bias = jnp.concatenate([bias_ref[...]] * stack, axis=0)
            scores = jnp.concatenate([scores[:, :128] + bias, scores[:, 128:]], axis=1)
        s_ref[slot, :, start:end] = scores
        return functools.reduce(jnp.maximum, lanes(scores, BIG))

    def finish(group, latent, lse, kept):
        for i in range(stack):
            part = slice(i * rows, (i + 1) * rows)
            head = group * stack + i
            at = slice(head * VDIM, (head + 1) * VDIM)
            value = jnp.dot(latent[part], wv_ref[head], preferred_element_type=F32)
            level = lse[part]
            if before:
                values, levels = [value], [level]
                for value_ref, level_ref in before:
                    values.append(value_ref[:, at])
                    chosen = jnp.where(lane == head, level_ref[...], 0.0)
                    levels.append(jnp.sum(chosen, axis=1, keepdims=True))
                best = functools.reduce(jnp.maximum, levels)
                shares = [jnp.exp2(x - best) for x in levels]
                whole = functools.reduce(jnp.add, shares)
                value = functools.reduce(jnp.add, [v * w for v, w in zip(values, shares)])
                value = value / whole
                level = best + jnp.log2(whole)
            out_ref[:, at] = value.astype(out_ref.dtype)
            kept = jnp.where(lane % 8 == head, level, kept)
        return kept

    def turn(group, kept, more):
        slot, other = group % 2, (group + 1) % 2
        top = jnp.max(top_ref[...], axis=1, keepdims=True)
        total = jnp.zeros((many, 128), F32)
        accum = None
        tops = []
        for start, end in cuts:
            weights = jnp.exp2(s_ref[slot, :, start:end] - top)
            for block in lanes(weights, 0.0):
                total = total + block
            mixed = jnp.dot(
                weights.astype(BF16), k_ref[start:end, :KV_RANK], preferred_element_type=F32
            )
            accum = mixed if accum is None else accum + mixed
            if more:
                tops.append(score(group + 1, other, (start, end)))
        if more:
            top_ref[...] = functools.reduce(jnp.maximum, tops)
        total = jnp.sum(total, axis=1, keepdims=True)
        return finish(group, (accum / total).astype(BF16), top + jnp.log2(total), kept)

    top_ref[...] = functools.reduce(jnp.maximum, [score(0, 0, cut) for cut in cuts])
    kept = jnp.zeros((rows, 128), F32)
    for group in range(groups):
        kept = turn(group, kept, group + 1 < groups)
    if kind != "packed":
        refs[1][...] = kept
        return
    high = kept.astype(BF16)
    rest = kept - high.astype(F32)
    mid = rest.astype(BF16)
    low = (rest - mid.astype(F32)).astype(BF16)
    out_ref[:, heads * VDIM :] = jnp.where(lane < 8, high, jnp.where(lane < 16, mid, low))


def attend(q, keys, w_uv, kind, bias=None, before=()):
    heads, rows, _ = q.shape
    count = keys.shape[0]
    stack = 4
    operands = [q, keys, w_uv]
    if bias is not None:
        operands.append(bias)
    for pair in before:
        operands += pair
    wide = heads * VDIM
    out_shape = [jax.ShapeDtypeStruct((rows, wide), F32), jax.ShapeDtypeStruct((rows, 128), F32)]
    if kind == "packed":
        out_shape = [jax.ShapeDtypeStruct((rows, wide + 128), BF16)]
    spec = pl.BlockSpec(memory_space=pltpu.VMEM)
    return pl.pallas_call(
        functools.partial(attend_kernel, stack, kind),
        in_specs=[spec] * len(operands),
        out_specs=[spec] * len(out_shape),
        out_shape=out_shape,
        scratch_shapes=[
            pltpu.VMEM((2, stack * rows, -(-count // 128) * 128), F32),
            pltpu.VMEM((stack * rows, 128), F32),
        ],
        compiler_params=pltpu.CompilerParams(vmem_limit_bytes=24 * 2**20),
        cost_estimate=pl.CostEstimate(
            flops=rows * heads * count * (WIDE + KV_RANK) // 8,
            bytes_accessed=2**19,
            transcendentals=0,
        ),
    )(*operands)


def prepare_kernel(kv_ref, cache_ref, gain_ref, cos_ref, sin_ref, run_ref, own_ref, keys_ref):
    core = lax.axis_index("head") % 2
    rows = kv_ref.shape[0]
    half = cache_ref.shape[0] // 2
    spare = WIDE - KV_RANK - ROPE
    latent = kv_ref[:, :KV_RANK].astype(F32)
    square = jnp.sum(latent * latent, axis=1, keepdims=True) / KV_RANK + 1e-06
    normed = latent / jnp.sqrt(square) * gain_ref[...]
    rope = kv_ref[:, KV_RANK:].astype(F32)
    swapped = jnp.concatenate([rope[:, ROPE // 2 :], rope[:, : ROPE // 2]], axis=1)
    rotated = rope * cos_ref[...] + swapped * sin_ref[...]
    slot = lax.broadcasted_iota(jnp.int32, (rows, spare), 1)
    one_hot = (run_ref[...] == slot).astype(F32)
    keys_ref[:rows, :KV_RANK] = normed.astype(BF16)
    keys_ref[:rows, KV_RANK:] = jnp.concatenate([rotated, one_hot], axis=1).astype(BF16)
    keys_ref[rows:, :KV_RANK] = cache_ref[:, :KV_RANK]
    keys_ref[rows:, KV_RANK:] = jnp.concatenate(
        [cache_ref[:, KV_RANK:], jnp.zeros((2 * half, spare), BF16)], axis=1
    )
    for i in range(2):

        @pl.when(core == i)
        def _():
            own_ref[:half] = keys_ref[rows + i * half : rows + (i + 1) * half]
            own_ref[half:] = keys_ref[i * RUN : (i + 1) * RUN]


def prepare(kv_new, cache, gain, cosine, sine, run):
    rows, old = kv_new.shape[0], cache.shape[0]
    spec = pl.BlockSpec(memory_space=pltpu.VMEM)
    return pl.pallas_call(
        prepare_kernel,
        in_specs=[spec] * 6,
        out_specs=[spec] * 2,
        out_shape=[
            jax.ShapeDtypeStruct(((rows + old) // 2, WIDE), BF16),
            jax.ShapeDtypeStruct((rows + old, WIDE), BF16),
        ],
        compiler_params=pltpu.CompilerParams(vmem_limit_bytes=16 * 2**20),
    )(kv_new, cache, gain, cosine, sine, run)


def tie(*arrays):
    return lax.optimization_barrier(arrays)


def step_z(a, b):
    return permute(b, SWAP_Z[0]), permute(a, SWAP_Z[1])


def both_cores(*pieces):
    mine = jnp.concatenate(pieces, axis=0)
    return mine, permute(mine, SWAP_CORE)


def turning(place):
    angle = angles(place.astype(F32), ROPE)
    cosine, sine = jnp.cos(angle), jnp.sin(angle)
    return jnp.concatenate([cosine, cosine], axis=1), jnp.concatenate([-sine, sine], axis=1)


def per_device(q_latent, kv_new, cache, latent_gain, positions, w_uq, w_uk, w_uv, w_out):
    rows = q_latent.shape[0]
    heads = w_uk.shape[0]
    head_index = lax.axis_index("head")
    seq_index = lax.axis_index("seq")
    core = head_index % 2
    x_hi = seq_index % 2
    spare = WIDE - KV_RANK - ROPE

    run = positions // RUN
    lane = jnp.arange(128)[None, :]
    marks = jnp.where(
        lane == 0, run[:, None], jnp.where(lane == 1, (positions % RUN)[:, None], 0)
    ).astype(BF16)
    other = permute(jnp.concatenate([q_latent, marks], axis=1), SWAP_MIRROR)

    cos_own, sin_own = turning(positions + PREFIX)
    own, keys_0 = prepare(
        kv_new, cache, latent_gain[None, :], cos_own, sin_own, run[:, None]
    )
    a_1, b_1 = step_z(own, own)
    mask = lambda r: jnp.where(jnp.arange(spare)[None, :] > r[:, None], BIG, 0.0).astype(BF16)
    q_own = queries(q_latent, w_uq, w_uk, cos_own, sin_own, mask(run))
    q_own, a_1, b_1 = tie(q_own, a_1, b_1)

    a_2, b_2 = step_z(a_1, b_1)
    mine_1, theirs_1 = both_cores(a_1, b_1)
    keys_1 = jnp.concatenate([keys_0, mine_1, theirs_1], axis=0)
    token = jnp.arange(rows)[:, None]
    hidden = (token // RUN == lane // RUN) & (lane % RUN > token % RUN)
    bias = jnp.where(hidden, BIG, 0.0).astype(F32)
    own_1 = attend(q_own, keys_1, w_uv, "first", bias=bias)
    own_1, a_2, b_2, other = tie(own_1, a_2, b_2, other)

    a_3, b_3 = step_z(a_2, b_2)
    mine_2, theirs_2 = both_cores(a_2, b_2)
    w_half = w_out.shape[0] // 2
    w_sent, other = tie(w_out[:w_half], other)
    w_first = permute(w_sent, SWAP_XH)
    other_marks = other[:, 1536:1538].astype(jnp.int32)
    other_run = other_marks[:, 0]
    cos_other, sin_other = turning(other_run * RUN + other_marks[:, 1] + PREFIX)
    q_other = queries(
        other[:, :1536], w_uq, w_uk, cos_other, sin_other, mask(other_run)
    )
    other_1 = attend(q_other, keys_1, w_uv, "next")
    other_1, a_3, b_3 = tie(other_1, a_3, b_3)

    half = a_3.shape[0] // 2
    a_4, b_4 = step_z(a_3[half:], b_3[:half])
    keys_2 = jnp.concatenate([mine_2, theirs_2], axis=0)
    other_2 = attend(q_other, keys_2, w_uv, "next")
    other_2, a_4, b_4, w_first = tie(other_2, a_4, b_4, w_first)
    mine_3, theirs_3 = both_cores(a_3, b_3, a_4, b_4)
    keys_3 = jnp.concatenate([mine_3, theirs_3], axis=0)
    (packed,) = attend(q_other, keys_3, w_uv, "packed", before=(other_1, other_2))
    came = permute(packed, SWAP_XH)
    q_own, packed = tie(q_own, packed)
    own_2 = attend(q_own, keys_2, w_uv, "next")
    merged, own_lse = attend(q_own, keys_3, w_uv, "own", before=(own_1, own_2))

    wide = heads * VDIM
    came_lse = sum(
        came[:, wide + i * heads : wide + (i + 1) * heads].astype(F32) for i in range(3)
    )
    own_lse = own_lse[:, :heads]
    best = jnp.maximum(own_lse, came_lse)
    own_weight = jnp.exp2(own_lse - best)
    came_weight = jnp.exp2(came_lse - best)
    both = own_weight + came_weight
    spread = lambda w: jnp.repeat(w / both, VDIM, axis=1)
    values = (
        merged * spread(own_weight) + came[:, :wide].astype(F32) * spread(came_weight)
    ).astype(BF16)

    z = seq_index // 2
    y = head_index // 4
    x_lo = (head_index // 2) % 2
    odd = z % 2

    def project(*blocks):
        block = jnp.concatenate(blocks, axis=0)
        send = jnp.dot(block, w_send, preferred_element_type=F32).astype(BF16)
        came = permute(send, SWAP_CORE)
        keep = jnp.dot(block, w_keep, preferred_element_type=F32)
        return (keep + came.astype(F32)).astype(BF16)

    def across(summed, swapped):
        def take(of):
            away = (of - z // 2) % 4
            side = jnp.where((away == 1) == (swapped == 1), 2, 1)
            at = jnp.where(away == 0, 0, jnp.where(away == 2, 3, side))
            return lax.dynamic_slice_in_dim(summed, at * rows, rows, 0)

        others = (y ^ 1, (y + jnp.where(y % 2 == 1, 1, 3)) % 4, y ^ 2)
        parts = [permute(take(of), swap) for of, swap in zip(others, SWAP_Y)]
        mine = take(y).astype(F32) + sum(p.astype(F32) for p in parts)
        return mine.astype(BF16)

    w_sent, values = tie(w_out[w_half:], values)
    w_second = permute(w_sent, SWAP_XH)
    a_1, b_1 = step_z(values, values)
    a_2, b_2 = step_z(a_1, b_1)
    a_2, b_2, w_second = tie(a_2, b_2, w_second)
    a_3, b_3 = step_z(a_2, b_2)
    same = x_hi == core
    w_other = jnp.concatenate([w_first, w_second], axis=0)
    w_keep = jnp.where(same, w_out, w_other)
    w_send = jnp.where(same, w_other, w_out)
    half = rows // 2
    a_4, b_4 = step_z(a_3[half:], b_3[:half])

    odd_wave = across(project(a_1, b_1, a_3, b_3), 1 - odd)
    even_wave = across(project(values, a_2, b_2, a_4, b_4), odd)

    even = x_lo == odd
    came = permute(jnp.where(even, odd_wave, even_wave), SWAP_XL)
    mine = jnp.where(even, even_wave, odd_wave)
    return permute((mine.astype(F32) + came.astype(F32)).astype(BF16), TO_PLACE)


def solution(mesh):
    placed = (
        P("seq", None),
        P("seq", None),
        P("seq", None),
        P(),
        P("seq"),
        P(None, "head"),
        P("head", None, None),
        P("head", None, None),
        P("head", "seq"),
    )
    return jax.shard_map(
        per_device, mesh=mesh, in_specs=placed, out_specs=P("seq", "head"), check_vma=False
    )
```

```python
import functools
import math

import jax
import jax.numpy as jnp
from jax import lax
from jax.experimental import pallas as pl
from jax.experimental.pallas import tpu as pltpu
from jax.sharding import PartitionSpec as P

KV_RANK = 512
ROPE = 64
NOPE = 128
VDIM = 128
RUN = 64
PREFIX = 3072
WIDE = 640
CHUNK = 512
AXES = ("seq", "head")
BIG = -1e30
F32 = jnp.float32
BF16 = jnp.bfloat16


def place_of(i):
    s, h = divmod(i, 16)
    return s // 2, s % 2, h // 4, (h // 2) % 2, h % 2


def index_of(z, xh, y, xl, c):
    return (z * 2 + xh) * 16 + y * 4 + xl * 2 + c


def pairs(to):
    moves = [(i, to(*place_of(i))) for i in range(256)]
    return [(i, index_of(*place)) for i, place in moves if place]


def next_to(i, size):
    return (i + 1 if i % 2 else i - 1) % size


SWAP_CORE = pairs(lambda z, xh, y, xl, c: (z, xh, y, xl, 1 - c))
SWAP_XH = pairs(lambda z, xh, y, xl, c: (z, 1 - xh, y, xl, c))
SWAP_MIRROR = pairs(lambda z, xh, y, xl, c: (z, 1 - xh, y, 1 - xl, c))
SWAP_Z = (
    pairs(lambda z, xh, y, xl, c: (z ^ 1, xh, y, xl, c)),
    pairs(lambda z, xh, y, xl, c: (next_to(z, 8), xh, y, xl, c)),
)
SWAP_Y = (
    pairs(lambda z, xh, y, xl, c: (z, xh, y ^ 1, xl, c)),
    pairs(lambda z, xh, y, xl, c: (z, xh, next_to(y, 4), xl, c)),
    pairs(lambda z, xh, y, xl, c: (z, xh, y ^ 2, xl, c)),
)


SWAP_XL = pairs(lambda z, xh, y, xl, c: (z, xh, y, 1 - xl, c))
TO_PLACE = pairs(lambda z, xh, y, xl, c: (2 * y + xl, xh, z >> 1, z & 1, c))


def permute(x, perm):
    return lax.ppermute(x, AXES, perm)


def angles(place, width):
    index = jnp.arange(width // 2, dtype=F32)
    inv_freq = jnp.exp(index * (-2.0 * math.log(10000.0) / width))
    return place[:, None] * inv_freq[None, :]


def query_kernel(lat_ref, wq_ref, wk_ref, cos_ref, sin_ref, mask_ref, out_ref):
    scale = (NOPE + ROPE) ** (-0.5) * math.log2(math.e)
    query = jnp.dot(lat_ref[...], wq_ref[...], preferred_element_type=F32).astype(BF16)
    for i in range(2):
        part = query[:, i * 192 : (i + 1) * 192]
        absorbed = jnp.dot(part[:, :NOPE], wk_ref[i], preferred_element_type=F32)
        out_ref[i, :, :KV_RANK] = (absorbed * scale).astype(BF16)
        rope = part[:, NOPE:].astype(F32)
        swapped = jnp.concatenate([rope[:, ROPE // 2 :], rope[:, : ROPE // 2]], axis=1)
        rotated = rope * cos_ref[...] + swapped * sin_ref[...]
        out_ref[i, :, KV_RANK:] = jnp.concatenate(
            [(rotated * scale).astype(BF16), mask_ref[...]], axis=1
        )


def queries(lat, w_uq, w_uk, cosine, sine, mask):
    rows = lat.shape[0]
    heads = w_uk.shape[0]
    whole = lambda i: (0, 0)
    return pl.pallas_call(
        query_kernel,
        grid=(heads // 2,),
        in_specs=[
            pl.BlockSpec(lat.shape, whole),
            pl.BlockSpec((w_uq.shape[0], 384), lambda i: (0, i)),
            pl.BlockSpec((2, NOPE, KV_RANK), lambda i: (i, 0, 0)),
            pl.BlockSpec(cosine.shape, whole),
            pl.BlockSpec(sine.shape, whole),
            pl.BlockSpec(mask.shape, whole),
        ],
        out_specs=pl.BlockSpec((2, rows, WIDE), lambda i: (i, 0, 0)),
        out_shape=jax.ShapeDtypeStruct((heads, rows, WIDE), BF16),
        compiler_params=pltpu.CompilerParams(vmem_limit_bytes=32 * 2**20),
        cost_estimate=pl.CostEstimate(
            flops=rows * heads * (1536 * 192 + 128 * 512) // 4,
            bytes_accessed=2**20,
            transcendentals=0,
        ),
    )(lat, w_uq, w_uk, cosine, sine, mask)


def lanes(x, fill):
    width = x.shape[1]
    blocks = [x[:, at : min(at + 128, width)] for at in range(0, width, 128)]
    short = 128 - blocks[-1].shape[1]
    if short:
        rest = jnp.full((x.shape[0], short), fill, x.dtype)
        blocks[-1] = jnp.concatenate([blocks[-1], rest], axis=1)
    return blocks


def attend_kernel(stack, kind, *refs):
    q_ref, k_ref, wv_ref = refs[:3]
    refs = list(refs[3:])
    bias_ref = refs.pop(0) if kind == "first" else None
    before = [(refs.pop(0), refs.pop(0)) for _ in range(2)] if kind in ("own", "packed") else []
    top_ref = refs.pop()
    s_ref = refs.pop()
    out_ref = refs[0]
    heads, rows, _ = q_ref.shape
    count = k_ref.shape[0]
    groups = heads // stack
    many = stack * rows
    cuts = [(at, min(at + CHUNK, count)) for at in range(0, count, CHUNK)]
    nt = (((1,), (1,)), ((), ()))
    lane = lax.broadcasted_iota(jnp.int32, (rows, 128), 1)

    def score(group, slot, cut):
        start, end = cut
        q = q_ref[pl.ds(group * stack, stack)].reshape(many, WIDE)
        scores = lax.dot_general(q, k_ref[start:end, :], nt, preferred_element_type=F32)
        if bias_ref is not None and start == 0:
            bias = jnp.concatenate([bias_ref[...]] * stack, axis=0)
            scores = jnp.concatenate([scores[:, :128] + bias, scores[:, 128:]], axis=1)
        s_ref[slot, :, start:end] = scores
        return functools.reduce(jnp.maximum, lanes(scores, BIG))

    def finish(group, latent, lse, kept):
        for i in range(stack):
            part = slice(i * rows, (i + 1) * rows)
            head = group * stack + i
            at = head * VDIM
            at = pl.ds(at if isinstance(at, int) else pl.multiple_of(at, VDIM), VDIM)
            value = jnp.dot(latent[part], wv_ref[head], preferred_element_type=F32)
            level = lse[part]
            if before:
                values, levels = [value], [level]
                for value_ref, level_ref in before:
                    values.append(value_ref[:, at])
                    chosen = jnp.where(lane == head, level_ref[...], 0.0)
                    levels.append(jnp.sum(chosen, axis=1, keepdims=True))
                best = functools.reduce(jnp.maximum, levels)
                shares = [jnp.exp2(x - best) for x in levels]
                whole = functools.reduce(jnp.add, shares)
                value = functools.reduce(jnp.add, [v * w for v, w in zip(values, shares)])
                value = value / whole
                level = best + jnp.log2(whole)
            out_ref[:, at] = value.astype(out_ref.dtype)
            kept = jnp.where(lane % 8 == head, level, kept)
        return kept

    def turn(group, kept, more):
        slot, other = group % 2, (group + 1) % 2
        top = jnp.max(top_ref[...], axis=1, keepdims=True)
        total = jnp.zeros((many, 128), F32)
        accum = None
        tops = []
        for start, end in cuts:
            weights = jnp.exp2(s_ref[slot, :, start:end] - top)
            for block in lanes(weights, 0.0):
                total = total + block
            mixed = jnp.dot(
                weights.astype(BF16), k_ref[start:end, :KV_RANK], preferred_element_type=F32
            )
            accum = mixed if accum is None else accum + mixed
            if more:
                tops.append(score(group + 1, other, (start, end)))
        if more:
            top_ref[...] = functools.reduce(jnp.maximum, tops)
        total = jnp.sum(total, axis=1, keepdims=True)
        return finish(group, (accum / total).astype(BF16), top + jnp.log2(total), kept)

    top_ref[...] = functools.reduce(jnp.maximum, [score(0, 0, cut) for cut in cuts])
    kept = lax.fori_loop(
        0, groups - 1, lambda g, kept: turn(g, kept, True), jnp.zeros((rows, 128), F32)
    )
    kept = turn(groups - 1, kept, False)
    if kind != "packed":
        refs[1][...] = kept
        return
    high = kept.astype(BF16)
    rest = kept - high.astype(F32)
    mid = rest.astype(BF16)
    low = (rest - mid.astype(F32)).astype(BF16)
    out_ref[:, heads * VDIM :] = jnp.where(lane < 8, high, jnp.where(lane < 16, mid, low))


def attend(q, keys, w_uv, kind, bias=None, before=()):
    heads, rows, _ = q.shape
    count = keys.shape[0]
    stack = 2
    operands = [q, keys, w_uv]
    if bias is not None:
        operands.append(bias)
    for pair in before:
        operands += pair
    wide = heads * VDIM
    out_shape = [jax.ShapeDtypeStruct((rows, wide), F32), jax.ShapeDtypeStruct((rows, 128), F32)]
    if kind == "packed":
        out_shape = [jax.ShapeDtypeStruct((rows, wide + 128), BF16)]
    spec = pl.BlockSpec(memory_space=pltpu.VMEM)
    return pl.pallas_call(
        functools.partial(attend_kernel, stack, kind),
        in_specs=[spec] * len(operands),
        out_specs=[spec] * len(out_shape),
        out_shape=out_shape,
        scratch_shapes=[
            pltpu.VMEM((2, stack * rows, -(-count // 128) * 128), F32),
            pltpu.VMEM((stack * rows, 128), F32),
        ],
        compiler_params=pltpu.CompilerParams(vmem_limit_bytes=24 * 2**20),
        cost_estimate=pl.CostEstimate(
            flops=rows * heads * count * (WIDE + KV_RANK) // 8,
            bytes_accessed=2**19,
            transcendentals=0,
        ),
    )(*operands)


def prepare_kernel(kv_ref, cache_ref, gain_ref, cos_ref, sin_ref, run_ref, own_ref, keys_ref):
    core = lax.axis_index("head") % 2
    rows = kv_ref.shape[0]
    half = cache_ref.shape[0] // 2
    spare = WIDE - KV_RANK - ROPE
    latent = kv_ref[:, :KV_RANK].astype(F32)
    square = jnp.sum(latent * latent, axis=1, keepdims=True) / KV_RANK + 1e-06
    normed = latent / jnp.sqrt(square) * gain_ref[...]
    rope = kv_ref[:, KV_RANK:].astype(F32)
    swapped = jnp.concatenate([rope[:, ROPE // 2 :], rope[:, : ROPE // 2]], axis=1)
    rotated = rope * cos_ref[...] + swapped * sin_ref[...]
    slot = lax.broadcasted_iota(jnp.int32, (rows, spare), 1)
    one_hot = (run_ref[...] == slot).astype(F32)
    keys_ref[:rows, :KV_RANK] = normed.astype(BF16)
    keys_ref[:rows, KV_RANK:] = jnp.concatenate([rotated, one_hot], axis=1).astype(BF16)
    keys_ref[rows:, :KV_RANK] = cache_ref[:, :KV_RANK]
    keys_ref[rows:, KV_RANK:] = jnp.concatenate(
        [cache_ref[:, KV_RANK:], jnp.zeros((2 * half, spare), BF16)], axis=1
    )
    for i in range(2):

        @pl.when(core == i)
        def _():
            own_ref[:half] = keys_ref[rows + i * half : rows + (i + 1) * half]
            own_ref[half:] = keys_ref[i * RUN : (i + 1) * RUN]


def prepare(kv_new, cache, gain, cosine, sine, run):
    rows, old = kv_new.shape[0], cache.shape[0]
    spec = pl.BlockSpec(memory_space=pltpu.VMEM)
    return pl.pallas_call(
        prepare_kernel,
        in_specs=[spec] * 6,
        out_specs=[spec] * 2,
        out_shape=[
            jax.ShapeDtypeStruct(((rows + old) // 2, WIDE), BF16),
            jax.ShapeDtypeStruct((rows + old, WIDE), BF16),
        ],
        compiler_params=pltpu.CompilerParams(vmem_limit_bytes=16 * 2**20),
    )(kv_new, cache, gain, cosine, sine, run)


def tie(*arrays):
    return lax.optimization_barrier(arrays)


def step_z(a, b):
    return permute(b, SWAP_Z[0]), permute(a, SWAP_Z[1])


def both_cores(*pieces):
    mine = jnp.concatenate(pieces, axis=0)
    return mine, permute(mine, SWAP_CORE)


def turning(place):
    angle = angles(place.astype(F32), ROPE)
    cosine, sine = jnp.cos(angle), jnp.sin(angle)
    return jnp.concatenate([cosine, cosine], axis=1), jnp.concatenate([-sine, sine], axis=1)


def per_device(q_latent, kv_new, cache, latent_gain, positions, w_uq, w_uk, w_uv, w_out):
    rows = q_latent.shape[0]
    heads = w_uk.shape[0]
    head_index = lax.axis_index("head")
    seq_index = lax.axis_index("seq")
    core = head_index % 2
    x_hi = seq_index % 2
    spare = WIDE - KV_RANK - ROPE

    run = positions // RUN
    lane = jnp.arange(128)[None, :]
    marks = jnp.where(
        lane == 0, run[:, None], jnp.where(lane == 1, (positions % RUN)[:, None], 0)
    ).astype(BF16)
    other = permute(jnp.concatenate([q_latent, marks], axis=1), SWAP_MIRROR)

    cos_own, sin_own = turning(positions + PREFIX)
    own, keys_0 = prepare(
        kv_new, cache, latent_gain[None, :], cos_own, sin_own, run[:, None]
    )
    a_1, b_1 = step_z(own, own)
    mask = lambda r: jnp.where(jnp.arange(spare)[None, :] > r[:, None], BIG, 0.0).astype(BF16)
    q_own = queries(q_latent, w_uq, w_uk, cos_own, sin_own, mask(run))
    q_own, a_1, b_1 = tie(q_own, a_1, b_1)

    a_2, b_2 = step_z(a_1, b_1)
    mine_1, theirs_1 = both_cores(a_1, b_1)
    keys_1 = jnp.concatenate([keys_0, mine_1, theirs_1], axis=0)
    token = jnp.arange(rows)[:, None]
    hidden = (token // RUN == lane // RUN) & (lane % RUN > token % RUN)
    bias = jnp.where(hidden, BIG, 0.0).astype(F32)
    own_1 = attend(q_own, keys_1, w_uv, "first", bias=bias)
    own_1, a_2, b_2, other = tie(own_1, a_2, b_2, other)

    a_3, b_3 = step_z(a_2, b_2)
    mine_2, theirs_2 = both_cores(a_2, b_2)
    w_half = w_out.shape[0] // 2
    w_sent, other = tie(w_out[:w_half], other)
    w_first = permute(w_sent, SWAP_XH)
    other_marks = other[:, 1536:1538].astype(jnp.int32)
    other_run = other_marks[:, 0]
    cos_other, sin_other = turning(other_run * RUN + other_marks[:, 1] + PREFIX)
    q_other = queries(
        other[:, :1536], w_uq, w_uk, cos_other, sin_other, mask(other_run)
    )
    other_1 = attend(q_other, keys_1, w_uv, "next")
    other_1, a_3, b_3 = tie(other_1, a_3, b_3)

    half = a_3.shape[0] // 2
    a_4, b_4 = step_z(a_3[half:], b_3[:half])
    keys_2 = jnp.concatenate([mine_2, theirs_2], axis=0)
    other_2 = attend(q_other, keys_2, w_uv, "next")
    other_2, a_4, b_4, w_first = tie(other_2, a_4, b_4, w_first)
    mine_3, theirs_3 = both_cores(a_3, b_3, a_4, b_4)
    keys_3 = jnp.concatenate([mine_3, theirs_3], axis=0)
    (packed,) = attend(q_other, keys_3, w_uv, "packed", before=(other_1, other_2))
    came = permute(packed, SWAP_XH)
    q_own, packed = tie(q_own, packed)
    own_2 = attend(q_own, keys_2, w_uv, "next")
    merged, own_lse = attend(q_own, keys_3, w_uv, "own", before=(own_1, own_2))

    wide = heads * VDIM
    came_lse = sum(
        came[:, wide + i * heads : wide + (i + 1) * heads].astype(F32) for i in range(3)
    )
    own_lse = own_lse[:, :heads]
    best = jnp.maximum(own_lse, came_lse)
    own_weight = jnp.exp2(own_lse - best)
    came_weight = jnp.exp2(came_lse - best)
    both = own_weight + came_weight
    spread = lambda w: jnp.repeat(w / both, VDIM, axis=1)
    values = (
        merged * spread(own_weight) + came[:, :wide].astype(F32) * spread(came_weight)
    ).astype(BF16)

    z = seq_index // 2
    y = head_index // 4
    x_lo = (head_index // 2) % 2
    odd = z % 2

    def project(*blocks):
        block = jnp.concatenate(blocks, axis=0)
        send = jnp.dot(block, w_send, preferred_element_type=F32).astype(BF16)
        came = permute(send, SWAP_CORE)
        keep = jnp.dot(block, w_keep, preferred_element_type=F32)
        return (keep + came.astype(F32)).astype(BF16)

    def across(summed, swapped):
        def take(of):
            away = (of - z // 2) % 4
            side = jnp.where((away == 1) == (swapped == 1), 2, 1)
            at = jnp.where(away == 0, 0, jnp.where(away == 2, 3, side))
            return lax.dynamic_slice_in_dim(summed, at * rows, rows, 0)

        others = (y ^ 1, (y + jnp.where(y % 2 == 1, 1, 3)) % 4, y ^ 2)
        parts = [permute(take(of), swap) for of, swap in zip(others, SWAP_Y)]
        mine = take(y).astype(F32) + sum(p.astype(F32) for p in parts)
        return mine.astype(BF16)

    w_sent, values = tie(w_out[w_half:], values)
    w_second = permute(w_sent, SWAP_XH)
    a_1, b_1 = step_z(values, values)
    a_2, b_2 = step_z(a_1, b_1)
    a_2, b_2, w_second = tie(a_2, b_2, w_second)
    a_3, b_3 = step_z(a_2, b_2)
    same = x_hi == core
    w_other = jnp.concatenate([w_first, w_second], axis=0)
    w_keep = jnp.where(same, w_out, w_other)
    w_send = jnp.where(same, w_other, w_out)
    half = rows // 2
    a_4, b_4 = step_z(a_3[half:], b_3[:half])

    odd_wave = across(project(a_1, b_1, a_3, b_3), 1 - odd)
    even_wave = across(project(values, a_2, b_2, a_4, b_4), odd)

    even = x_lo == odd
    came = permute(jnp.where(even, odd_wave, even_wave), SWAP_XL)
    mine = jnp.where(even, even_wave, odd_wave)
    return permute((mine.astype(F32) + came.astype(F32)).astype(BF16), TO_PLACE)


def solution(mesh):
    placed = (
        P("seq", None),
        P("seq", None),
        P("seq", None),
        P(),
        P("seq"),
        P(None, "head"),
        P("head", None, None),
        P("head", None, None),
        P("head", "seq"),
    )
    return jax.shard_map(
        per_device, mesh=mesh, in_specs=placed, out_specs=P("seq", "head"), check_vma=False
    )
```

```python
import functools
import math

import jax
import jax.numpy as jnp
from jax import lax
from jax.experimental import pallas as pl
from jax.experimental.pallas import tpu as pltpu
from jax.sharding import PartitionSpec as P

KV_RANK = 512
ROPE = 64
NOPE = 128
VDIM = 128
RUN = 64
PREFIX = 3072
WIDE = 640
CHUNK = 512
AXES = ("seq", "head")
BIG = -1e30
F32 = jnp.float32
BF16 = jnp.bfloat16


def place_of(i):
    s, h = divmod(i, 16)
    return s // 2, s % 2, h // 4, (h // 2) % 2, h % 2


def index_of(z, xh, y, xl, c):
    return (z * 2 + xh) * 16 + y * 4 + xl * 2 + c


def pairs(to):
    moves = [(i, to(*place_of(i))) for i in range(256)]
    return [(i, index_of(*place)) for i, place in moves if place]


def next_to(i, size):
    return (i + 1 if i % 2 else i - 1) % size


SWAP_CORE = pairs(lambda z, xh, y, xl, c: (z, xh, y, xl, 1 - c))
SWAP_XH = pairs(lambda z, xh, y, xl, c: (z, 1 - xh, y, xl, c))
SWAP_MIRROR = pairs(lambda z, xh, y, xl, c: (z, 1 - xh, y, 1 - xl, c))
SWAP_Z = (
    pairs(lambda z, xh, y, xl, c: (z ^ 1, xh, y, xl, c)),
    pairs(lambda z, xh, y, xl, c: (next_to(z, 8), xh, y, xl, c)),
)
SWAP_Y = (
    pairs(lambda z, xh, y, xl, c: (z, xh, y ^ 1, xl, c)),
    pairs(lambda z, xh, y, xl, c: (z, xh, next_to(y, 4), xl, c)),
    pairs(lambda z, xh, y, xl, c: (z, xh, y ^ 2, xl, c)),
)


SWAP_XL = pairs(lambda z, xh, y, xl, c: (z, xh, y, 1 - xl, c))
TO_PLACE = pairs(lambda z, xh, y, xl, c: (2 * y + xl, xh, z >> 1, z & 1, c))


def permute(x, perm):
    return lax.ppermute(x, AXES, perm)


def angles(place, width):
    index = jnp.arange(width // 2, dtype=F32)
    inv_freq = jnp.exp(index * (-2.0 * math.log(10000.0) / width))
    return place[:, None] * inv_freq[None, :]


def query_kernel(lat_ref, wq_ref, wk_ref, cos_ref, sin_ref, mask_ref, out_ref):
    scale = (NOPE + ROPE) ** (-0.5) * math.log2(math.e)
    query = jnp.dot(lat_ref[...], wq_ref[...], preferred_element_type=F32).astype(BF16)
    for i in range(2):
        part = query[:, i * 192 : (i + 1) * 192]
        absorbed = jnp.dot(part[:, :NOPE], wk_ref[i], preferred_element_type=F32)
        out_ref[i, :, :KV_RANK] = (absorbed * scale).astype(BF16)
        rope = part[:, NOPE:].astype(F32)
        swapped = jnp.concatenate([rope[:, ROPE // 2 :], rope[:, : ROPE // 2]], axis=1)
        rotated = rope * cos_ref[...] + swapped * sin_ref[...]
        out_ref[i, :, KV_RANK:] = jnp.concatenate(
            [(rotated * scale).astype(BF16), mask_ref[...]], axis=1
        )


def queries(lat, w_uq, w_uk, cosine, sine, mask):
    rows = lat.shape[0]
    heads = w_uk.shape[0]
    whole = lambda i: (0, 0)
    return pl.pallas_call(
        query_kernel,
        grid=(heads // 2,),
        in_specs=[
            pl.BlockSpec(lat.shape, whole),
            pl.BlockSpec((w_uq.shape[0], 384), lambda i: (0, i)),
            pl.BlockSpec((2, NOPE, KV_RANK), lambda i: (i, 0, 0)),
            pl.BlockSpec(cosine.shape, whole),
            pl.BlockSpec(sine.shape, whole),
            pl.BlockSpec(mask.shape, whole),
        ],
        out_specs=pl.BlockSpec((2, rows, WIDE), lambda i: (i, 0, 0)),
        out_shape=jax.ShapeDtypeStruct((heads, rows, WIDE), BF16),
        compiler_params=pltpu.CompilerParams(vmem_limit_bytes=32 * 2**20),
        cost_estimate=pl.CostEstimate(
            flops=rows * heads * (1536 * 192 + 128 * 512) // 4,
            bytes_accessed=2**20,
            transcendentals=0,
        ),
    )(lat, w_uq, w_uk, cosine, sine, mask)


def lanes(x, fill):
    width = x.shape[1]
    blocks = [x[:, at : min(at + 128, width)] for at in range(0, width, 128)]
    short = 128 - blocks[-1].shape[1]
    if short:
        rest = jnp.full((x.shape[0], short), fill, x.dtype)
        blocks[-1] = jnp.concatenate([blocks[-1], rest], axis=1)
    return blocks


def attend_kernel(stack, kind, *refs):
    q_ref, k_ref, wv_ref = refs[:3]
    refs = list(refs[3:])
    bias_ref = refs.pop(0) if kind == "first" else None
    before = [(refs.pop(0), refs.pop(0)) for _ in range(2)] if kind in ("own", "packed") else []
    top_ref = refs.pop()
    s_ref = refs.pop()
    out_ref = refs[0]
    heads, rows, _ = q_ref.shape
    count = k_ref.shape[0]
    groups = heads // stack
    many = stack * rows
    cuts = [(at, min(at + CHUNK, count)) for at in range(0, count, CHUNK)]
    nt = (((1,), (1,)), ((), ()))
    lane = lax.broadcasted_iota(jnp.int32, (rows, 128), 1)

    def score(group, slot, cut):
        start, end = cut
        q = q_ref[pl.ds(group * stack, stack)].reshape(many, WIDE)
        scores = lax.dot_general(q, k_ref[start:end, :], nt, preferred_element_type=F32)
        if bias_ref is not None and start == 0:
            bias = jnp.concatenate([bias_ref[...]] * stack, axis=0)
            scores = jnp.concatenate([scores[:, :128] + bias, scores[:, 128:]], axis=1)
        s_ref[slot, :, start:end] = scores
        return functools.reduce(jnp.maximum, lanes(scores, BIG))

    def finish(group, latent, lse, kept):
        for i in range(stack):
            part = slice(i * rows, (i + 1) * rows)
            head = group * stack + i
            at = head * VDIM
            at = pl.ds(at if isinstance(at, int) else pl.multiple_of(at, VDIM), VDIM)
            value = jnp.dot(latent[part], wv_ref[head], preferred_element_type=F32)
            level = lse[part]
            if before:
                values, levels = [value], [level]
                for value_ref, level_ref in before:
                    values.append(value_ref[:, at])
                    chosen = jnp.where(lane == head, level_ref[...], 0.0)
                    levels.append(jnp.sum(chosen, axis=1, keepdims=True))
                best = functools.reduce(jnp.maximum, levels)
                shares = [jnp.exp2(x - best) for x in levels]
                whole = functools.reduce(jnp.add, shares)
                value = functools.reduce(jnp.add, [v * w for v, w in zip(values, shares)])
                value = value / whole
                level = best + jnp.log2(whole)
            out_ref[:, at] = value.astype(out_ref.dtype)
            kept = jnp.where(lane % 8 == head, level, kept)
        return kept

    def turn(group, kept, more):
        slot, other = group % 2, (group + 1) % 2
        top = jnp.max(top_ref[...], axis=1, keepdims=True)
        total = jnp.zeros((many, 128), F32)
        accum = None
        tops = []
        for start, end in cuts:
            weights = jnp.exp2(s_ref[slot, :, start:end] - top)
            for block in lanes(weights, 0.0):
                total = total + block
            mixed = jnp.dot(
                weights.astype(BF16), k_ref[start:end, :KV_RANK], preferred_element_type=F32
            )
            accum = mixed if accum is None else accum + mixed
            if more:
                tops.append(score(group + 1, other, (start, end)))
        if more:
            top_ref[...] = functools.reduce(jnp.maximum, tops)
        total = jnp.sum(total, axis=1, keepdims=True)
        return finish(group, (accum / total).astype(BF16), top + jnp.log2(total), kept)

    top_ref[...] = functools.reduce(jnp.maximum, [score(0, 0, cut) for cut in cuts])
    kept = jnp.zeros((rows, 128), F32)
    if groups == 2:
        kept = turn(0, kept, True)
    else:
        kept = lax.fori_loop(0, groups - 1, lambda g, kept: turn(g, kept, True), kept)
    kept = turn(groups - 1, kept, False)
    if kind != "packed":
        refs[1][...] = kept
        return
    high = kept.astype(BF16)
    rest = kept - high.astype(F32)
    mid = rest.astype(BF16)
    low = (rest - mid.astype(F32)).astype(BF16)
    out_ref[:, heads * VDIM :] = jnp.where(lane < 8, high, jnp.where(lane < 16, mid, low))


def attend(q, keys, w_uv, kind, bias=None, before=()):
    heads, rows, _ = q.shape
    count = keys.shape[0]
    stack = 4 if kind == "packed" else 2
    operands = [q, keys, w_uv]
    if bias is not None:
        operands.append(bias)
    for pair in before:
        operands += pair
    wide = heads * VDIM
    out_shape = [jax.ShapeDtypeStruct((rows, wide), F32), jax.ShapeDtypeStruct((rows, 128), F32)]
    if kind == "packed":
        out_shape = [jax.ShapeDtypeStruct((rows, wide + 128), BF16)]
    spec = pl.BlockSpec(memory_space=pltpu.VMEM)
    return pl.pallas_call(
        functools.partial(attend_kernel, stack, kind),
        in_specs=[spec] * len(operands),
        out_specs=[spec] * len(out_shape),
        out_shape=out_shape,
        scratch_shapes=[
            pltpu.VMEM((2, stack * rows, -(-count // 128) * 128), F32),
            pltpu.VMEM((stack * rows, 128), F32),
        ],
        compiler_params=pltpu.CompilerParams(vmem_limit_bytes=24 * 2**20),
        cost_estimate=pl.CostEstimate(
            flops=rows * heads * count * (WIDE + KV_RANK) // 8,
            bytes_accessed=2**19,
            transcendentals=0,
        ),
    )(*operands)


def prepare_kernel(kv_ref, cache_ref, gain_ref, cos_ref, sin_ref, run_ref, own_ref, keys_ref):
    core = lax.axis_index("head") % 2
    rows = kv_ref.shape[0]
    half = cache_ref.shape[0] // 2
    spare = WIDE - KV_RANK - ROPE
    latent = kv_ref[:, :KV_RANK].astype(F32)
    square = jnp.sum(latent * latent, axis=1, keepdims=True) / KV_RANK + 1e-06
    normed = latent / jnp.sqrt(square) * gain_ref[...]
    rope = kv_ref[:, KV_RANK:].astype(F32)
    swapped = jnp.concatenate([rope[:, ROPE // 2 :], rope[:, : ROPE // 2]], axis=1)
    rotated = rope * cos_ref[...] + swapped * sin_ref[...]
    slot = lax.broadcasted_iota(jnp.int32, (rows, spare), 1)
    one_hot = (run_ref[...] == slot).astype(F32)
    keys_ref[:rows, :KV_RANK] = normed.astype(BF16)
    keys_ref[:rows, KV_RANK:] = jnp.concatenate([rotated, one_hot], axis=1).astype(BF16)
    keys_ref[rows:, :KV_RANK] = cache_ref[:, :KV_RANK]
    keys_ref[rows:, KV_RANK:] = jnp.concatenate(
        [cache_ref[:, KV_RANK:], jnp.zeros((2 * half, spare), BF16)], axis=1
    )
    for i in range(2):

        @pl.when(core == i)
        def _():
            own_ref[:half] = keys_ref[rows + i * half : rows + (i + 1) * half]
            own_ref[half:] = keys_ref[i * RUN : (i + 1) * RUN]


def prepare(kv_new, cache, gain, cosine, sine, run):
    rows, old = kv_new.shape[0], cache.shape[0]
    spec = pl.BlockSpec(memory_space=pltpu.VMEM)
    return pl.pallas_call(
        prepare_kernel,
        in_specs=[spec] * 6,
        out_specs=[spec] * 2,
        out_shape=[
            jax.ShapeDtypeStruct(((rows + old) // 2, WIDE), BF16),
            jax.ShapeDtypeStruct((rows + old, WIDE), BF16),
        ],
        compiler_params=pltpu.CompilerParams(vmem_limit_bytes=16 * 2**20),
    )(kv_new, cache, gain, cosine, sine, run)


def tie(*arrays):
    return lax.optimization_barrier(arrays)


def step_z(a, b):
    return permute(b, SWAP_Z[0]), permute(a, SWAP_Z[1])


def both_cores(*pieces):
    mine = jnp.concatenate(pieces, axis=0)
    return mine, permute(mine, SWAP_CORE)


def turning(place):
    angle = angles(place.astype(F32), ROPE)
    cosine, sine = jnp.cos(angle), jnp.sin(angle)
    return jnp.concatenate([cosine, cosine], axis=1), jnp.concatenate([-sine, sine], axis=1)


def per_device(q_latent, kv_new, cache, latent_gain, positions, w_uq, w_uk, w_uv, w_out):
    rows = q_latent.shape[0]
    heads = w_uk.shape[0]
    head_index = lax.axis_index("head")
    seq_index = lax.axis_index("seq")
    core = head_index % 2
    x_hi = seq_index % 2
    spare = WIDE - KV_RANK - ROPE

    run = positions // RUN
    lane = jnp.arange(128)[None, :]
    marks = jnp.where(
        lane == 0, run[:, None], jnp.where(lane == 1, (positions % RUN)[:, None], 0)
    ).astype(BF16)
    other = permute(jnp.concatenate([q_latent, marks], axis=1), SWAP_MIRROR)

    cos_own, sin_own = turning(positions + PREFIX)
    own, keys_0 = prepare(
        kv_new, cache, latent_gain[None, :], cos_own, sin_own, run[:, None]
    )
    a_1, b_1 = step_z(own, own)
    mask = lambda r: jnp.where(jnp.arange(spare)[None, :] > r[:, None], BIG, 0.0).astype(BF16)
    q_own = queries(q_latent, w_uq, w_uk, cos_own, sin_own, mask(run))
    q_own, a_1, b_1 = tie(q_own, a_1, b_1)

    a_2, b_2 = step_z(a_1, b_1)
    mine_1, theirs_1 = both_cores(a_1, b_1)
    keys_1 = jnp.concatenate([keys_0, mine_1, theirs_1], axis=0)
    token = jnp.arange(rows)[:, None]
    hidden = (token // RUN == lane // RUN) & (lane % RUN > token % RUN)
    bias = jnp.where(hidden, BIG, 0.0).astype(F32)
    own_1 = attend(q_own, keys_1, w_uv, "first", bias=bias)
    own_1, a_2, b_2, other = tie(own_1, a_2, b_2, other)

    a_3, b_3 = step_z(a_2, b_2)
    mine_2, theirs_2 = both_cores(a_2, b_2)
    w_half = w_out.shape[0] // 2
    w_sent, other = tie(w_out[:w_half], other)
    w_first = permute(w_sent, SWAP_XH)
    other_marks = other[:, 1536:1538].astype(jnp.int32)
    other_run = other_marks[:, 0]
    cos_other, sin_other = turning(other_run * RUN + other_marks[:, 1] + PREFIX)
    q_other = queries(
        other[:, :1536], w_uq, w_uk, cos_other, sin_other, mask(other_run)
    )
    other_1 = attend(q_other, keys_1, w_uv, "next")
    other_1, a_3, b_3 = tie(other_1, a_3, b_3)

    half = a_3.shape[0] // 2
    a_4, b_4 = step_z(a_3[half:], b_3[:half])
    keys_2 = jnp.concatenate([mine_2, theirs_2], axis=0)
    other_2 = attend(q_other, keys_2, w_uv, "next")
    other_2, a_4, b_4, w_first = tie(other_2, a_4, b_4, w_first)
    mine_3, theirs_3 = both_cores(a_3, b_3, a_4, b_4)
    keys_3 = jnp.concatenate([mine_3, theirs_3], axis=0)
    (packed,) = attend(q_other, keys_3, w_uv, "packed", before=(other_1, other_2))
    came = permute(packed, SWAP_XH)
    q_own, packed = tie(q_own, packed)
    own_2 = attend(q_own, keys_2, w_uv, "next")
    merged, own_lse = attend(q_own, keys_3, w_uv, "own", before=(own_1, own_2))

    wide = heads * VDIM
    came_lse = sum(
        came[:, wide + i * heads : wide + (i + 1) * heads].astype(F32) for i in range(3)
    )
    own_lse = own_lse[:, :heads]
    best = jnp.maximum(own_lse, came_lse)
    own_weight = jnp.exp2(own_lse - best)
    came_weight = jnp.exp2(came_lse - best)
    both = own_weight + came_weight
    spread = lambda w: jnp.repeat(w / both, VDIM, axis=1)
    values = (
        merged * spread(own_weight) + came[:, :wide].astype(F32) * spread(came_weight)
    ).astype(BF16)

    z = seq_index // 2
    y = head_index // 4
    x_lo = (head_index // 2) % 2
    odd = z % 2

    def project(*blocks):
        block = jnp.concatenate(blocks, axis=0)
        send = jnp.dot(block, w_send, preferred_element_type=F32).astype(BF16)
        came = permute(send, SWAP_CORE)
        keep = jnp.dot(block, w_keep, preferred_element_type=F32)
        return (keep + came.astype(F32)).astype(BF16)

    def across(summed, swapped):
        def take(of):
            away = (of - z // 2) % 4
            side = jnp.where((away == 1) == (swapped == 1), 2, 1)
            at = jnp.where(away == 0, 0, jnp.where(away == 2, 3, side))
            return lax.dynamic_slice_in_dim(summed, at * rows, rows, 0)

        others = (y ^ 1, (y + jnp.where(y % 2 == 1, 1, 3)) % 4, y ^ 2)
        parts = [permute(take(of), swap) for of, swap in zip(others, SWAP_Y)]
        mine = take(y).astype(F32) + sum(p.astype(F32) for p in parts)
        return mine.astype(BF16)

    w_sent, values = tie(w_out[w_half:], values)
    w_second = permute(w_sent, SWAP_XH)
    a_1, b_1 = step_z(values, values)
    a_2, b_2 = step_z(a_1, b_1)
    a_2, b_2, w_second = tie(a_2, b_2, w_second)
    a_3, b_3 = step_z(a_2, b_2)
    same = x_hi == core
    w_other = jnp.concatenate([w_first, w_second], axis=0)
    w_keep = jnp.where(same, w_out, w_other)
    w_send = jnp.where(same, w_other, w_out)
    half = rows // 2
    a_4, b_4 = step_z(a_3[half:], b_3[:half])

    odd_wave = across(project(a_1, b_1, a_3, b_3), 1 - odd)
    even_wave = across(project(values, a_2, b_2, a_4, b_4), odd)

    even = x_lo == odd
    came = permute(jnp.where(even, odd_wave, even_wave), SWAP_XL)
    mine = jnp.where(even, even_wave, odd_wave)
    return permute((mine.astype(F32) + came.astype(F32)).astype(BF16), TO_PLACE)


def solution(mesh):
    placed = (
        P("seq", None),
        P("seq", None),
        P("seq", None),
        P(),
        P("seq"),
        P(None, "head"),
        P("head", None, None),
        P("head", None, None),
        P("head", "seq"),
    )
    return jax.shard_map(
        per_device, mesh=mesh, in_specs=placed, out_specs=P("seq", "head"), check_vma=False
    )
```
